32 devices in a mesh: groups: 2 (over x), dp: 16 (over z, y, core).
Axes of the slice: x: 2, y: 2, z: 4, core: 2. Of those that a mesh axis runs over, the one named last changes fastest.
Arguments:
- points: bfloat16 [131072, 128], P(('groups', 'dp')), parts along dimension 0, may hold values from -0.52 to 0.52
- probes: bfloat16 [16, 131072], P(None, ('groups', 'dp')), parts along dimension 1, may hold values from -6 to 6
- round_masks: int32 [6], P('groups'), parts along dimension 0, may hold values from 1 to 15, as said below
Outputs:
- product: float32 [16, 131072], P(None, ('groups', 'dp')), parts along dimension 1
The draws below stay inside these ranges and needn't reach their ends.
There are 2 independent parts, one for each index of `groups`. The reference program is written for one: setup_inputs(seed, part) draws one part's arguments, and reference() takes and returns one part's arrays. A program takes and returns all parts, laid end to end along the dimension named above; each array names one. Nothing has to cross between parts.
Inputs may be any that keep to these rules, and one draw needn't show every extreme that they name: `round_masks`: the 3 masks are distinct; one of them equals 15.
All inputs are finite; a program needn't handle non-finite values.
Results may differ from the reference program's by a relative error of at most 0.0028.
Values may be sent and summed in bfloat16 or wider, within the bound.
A program may use at most 64 MiB of HBM per device.

```python
import jax
import jax.numpy as jnp
from jax import lax

D = 128
PROBES = 16
PTS_DEV = 4096
ROUNDS = 3
POINTS = 65536
N_DP = 16


def draw_points(key, part):
    key = jax.random.fold_in(key, 5)
    key_base, key_centre, key_member, key_noise = jax.random.split(key, 4)
    base = jnp.clip(0.088 * jax.random.normal(key_base, (POINTS, D), jnp.float32), -0.5, 0.5)
    centres = jnp.clip(0.19 * jax.random.normal(key_centre, (4, D), jnp.float32), -0.45, 0.45)
    noise = 0.03 * jax.random.normal(key_noise, (POINTS, D), jnp.float32)
    chosen = jax.random.randint(key_member, (POINTS,), 0, 100)
    member = chosen < 4
    which = chosen % 4
    picked = jnp.zeros((POINTS, D), jnp.float32)
    for cluster in range(4):
        picked = jnp.where((which == cluster)[:, None], centres[cluster][None, :], picked)
    rows = jnp.where(member[:, None], picked + noise, base)
    return jnp.clip(rows, -0.52, 0.52).astype(jnp.bfloat16)


def draw_round_masks(key, part):
    key = jax.random.fold_in(key, 11)
    first, second = jax.random.split(key)
    others = jax.random.permutation(first, N_DP - 2) + 1
    picked = jnp.concatenate([others[:ROUNDS - 1], jnp.array([N_DP - 1], dtype=jnp.int32)])
    order = jax.random.permutation(second, ROUNDS)
    return picked[order].astype(jnp.int32)


def level_of(stream_key, extent, pieces, least, top_value):
    loudness, own = 1.0, jax.random.fold_in(stream_key, 6)
    for dim, blocks in pieces:
        heights = jnp.exp(jax.random.uniform(jax.random.fold_in(own, dim), (blocks,), jnp.float32, least / len(pieces), top_value / len(pieces)))
        loudness = loudness * jnp.repeat(heights, extent[dim] // blocks).reshape([-1 if axis == dim else 1 for axis in range(len(extent))])
    return loudness


def bell_draw(stream_key, dims, width, bound, pieces=(), held_as=jnp.bfloat16):
    gain = level_of(stream_key, dims, pieces, -0.22, 0.18) if pieces else 1.0
    drawn = jax.random.normal(stream_key, dims, jnp.float32) * width * gain
    return jnp.minimum(jnp.maximum(drawn, -bound), bound).astype(held_as)


def setup_inputs(seed: int = 0, part: int = 0) -> dict:
    keys = jax.random.split(jax.random.key(seed), 4)
    part_splits = jax.random.split(jax.random.fold_in(keys[3], part), 4)
    return {
        "points": draw_points(jax.random.fold_in(jax.random.fold_in(keys[3], part), 71), part),
        "probes": bell_draw(part_splits[1], (PROBES, POINTS), 1.0, 6.0, ((1, 16),)),
        "round_masks": draw_round_masks(jax.random.fold_in(jax.random.fold_in(keys[3], part), 71), part),
    }


GAMMA = 2.0
NOISE = 0.25


def reference(points, probes, round_masks):
    norms = jnp.sum(jnp.square(points.astype(jnp.float32)), axis=1)

    def one_block(block):
        start = (block * PTS_DEV).astype(jnp.int32)
        own_x = lax.dynamic_slice(points, (start, jnp.int32(0)), (PTS_DEV, D))
        own_n = lax.dynamic_slice(norms, (start,), (PTS_DEV,))
        own_v = lax.dynamic_slice(probes, (jnp.int32(0), start), (PROBES, PTS_DEV))
        total = NOISE * own_v.astype(jnp.float32)
        partners = [block] + [jnp.bitwise_xor(block, round_masks[r]) for r in range(ROUNDS)]
        for partner in partners:
            other = (partner * PTS_DEV).astype(jnp.int32)
            far_x = lax.dynamic_slice(points, (other, jnp.int32(0)), (PTS_DEV, D))
            far_n = lax.dynamic_slice(norms, (other,), (PTS_DEV,))
            far_v = lax.dynamic_slice(probes, (jnp.int32(0), other), (PROBES, PTS_DEV))
            dots = jnp.dot(own_x, far_x.T, preferred_element_type=jnp.float32)
            kern = jnp.exp(-GAMMA * (own_n[:, None] + far_n[None, :] - 2.0 * dots)).astype(jnp.bfloat16)
            total = total + jnp.dot(far_v, kern.T, preferred_element_type=jnp.float32)
        return total

    blocks = lax.map(one_block, jnp.arange(N_DP, dtype=jnp.int32))
    return blocks.transpose(1, 0, 2).reshape(PROBES, N_DP * PTS_DEV)
```

```python
import functools

import jax
import jax.numpy as jnp
from jax import lax
from jax.experimental import pallas as pl
from jax.experimental.pallas import tpu as pltpu
from jax.sharding import PartitionSpec as P

GAMMA = 2.0
NOISE = 0.25
F32, BF = jnp.float32, jnp.bfloat16


def extend(x_ref, out_ref, scale, own):
    rows, width = x_ref.shape
    chunk = 256

    def step(c, carry):
        r = pl.ds(pl.multiple_of(c * chunk, chunk), chunk)
        xf = x_ref[r, :].astype(F32)
        n = -GAMMA * jnp.sum(xf * xf, axis=1, keepdims=True)
        nh = n.astype(BF).astype(F32)
        rest = n - nh
        nm = rest.astype(BF).astype(F32)
        nl = rest - nm
        lane = lax.broadcasted_iota(jnp.int32, (chunk, 128), 1)
        o = 0 if own else 3
        p = 3 - o
        ones = jnp.where((lane >= p) & (lane < p + 3), 1.0, 0.0)
        extra = jnp.where(
            lane == o,
            nh,
            jnp.where(lane == o + 1, nm, jnp.where(lane == o + 2, nl, ones)),
        )
        out_ref[r, 0:width] = (xf * scale).astype(BF)
        out_ref[r, width : width + 128] = extra.astype(BF)
        return carry

    lax.fori_loop(0, rows // chunk, step, 0)


def tile_kernel(block_i, block_j, idx_ref, far_ref, own_ref, v_ref, start_ref, o_ref, oext, fext):
    rows = own_ref.shape[0]

    @pl.when(pl.program_id(0) == 0)
    def _():
        extend(own_ref, oext, 2 * GAMMA, True)
        o_ref[...] = start_ref[...]

    extend(far_ref, fext, 1.0, False)

    def istep(i, carry):
        ri = pl.ds(pl.multiple_of(i * block_i, block_i), block_i)
        w = oext[ri, :]
        a = o_ref[:, ri]
        for j in range(rows // block_j):
            rj = pl.ds(j * block_j, block_j)
            z = lax.dot_general(
                fext[rj, :], w, (((1,), (1,)), ((), ())), preferred_element_type=F32
            )
            k = jnp.exp(z).astype(BF)
            a = a + jnp.dot(v_ref[:, rj], k, preferred_element_type=F32)
        o_ref[:, ri] = a
        return carry

    lax.fori_loop(0, rows // block_i, istep, 0)


def tiles(idx, far, own, v, start):
    rows, width = own.shape
    probes = start.shape[0]
    count = idx.shape[0]
    n = count * rows * rows
    return pl.pallas_call(
        functools.partial(tile_kernel, 256, 1024),
        out_shape=jax.ShapeDtypeStruct((probes, rows), F32),
        grid_spec=pltpu.PrefetchScalarGridSpec(
            num_scalar_prefetch=1,
            grid=(count,),
            in_specs=[
                pl.BlockSpec((rows, width), lambda t, m: (m[t], 0)),
                pl.BlockSpec((rows, width), lambda t, m: (0, 0)),
                pl.BlockSpec((probes, rows), lambda t, m: (m[t], 0)),
                pl.BlockSpec((probes, rows), lambda t, m: (0, 0)),
            ],
            out_specs=pl.BlockSpec((probes, rows), lambda t, m: (0, 0)),
            scratch_shapes=[
                pltpu.VMEM((rows, width + 128), BF),
                pltpu.VMEM((rows, width + 128), BF),
            ],
        ),
        compiler_params=pltpu.CompilerParams(vmem_limit_bytes=40 << 20),
        cost_estimate=pl.CostEstimate(
            flops=2 * n * (2 * width + 256), bytes_accessed=count * rows * width * 2, transcendentals=n
        ),
    )(idx, far, own, v, start)


def on_device(points, probes, round_masks):
    me = lax.axis_index("dp")
    all_x = lax.all_gather(points, "dp", axis=0, tiled=True)
    all_v = lax.all_gather(probes, "dp", axis=0, tiled=True)
    zero = jnp.zeros((1,), jnp.int32)
    total = tiles(zero, points, points, probes, NOISE * probes.astype(F32))
    return tiles(jnp.bitwise_xor(me, round_masks), all_x, points, all_v, total)


def solution(mesh):
    in_specs = (P(("groups", "dp"), None), P(None, ("groups", "dp")), P("groups"))
    out_specs = P(None, ("groups", "dp"))
    return jax.shard_map(
        on_device, mesh=mesh, in_specs=in_specs, out_specs=out_specs, check_vma=False
    )
```

```python
import functools

import jax
import jax.numpy as jnp
from jax import lax
from jax.experimental import pallas as pl
from jax.experimental.pallas import tpu as pltpu
from jax.sharding import PartitionSpec as P

GAMMA = 2.0
NOISE = 0.25
F32, BF = jnp.float32, jnp.bfloat16
BLOCK_I = 512


def extended(x, scale, own):
    xf = x.astype(F32)
    n = -GAMMA * jnp.sum(xf * xf, axis=1, keepdims=True)
    nh = n.astype(BF).astype(F32)
    rest = n - nh
    nm = rest.astype(BF).astype(F32)
    nl = rest - nm
    lane = lax.broadcasted_iota(jnp.int32, (x.shape[0], 128), 1)
    o = 0 if own else 3
    p = 3 - o
    ones = jnp.where((lane >= p) & (lane < p + 3), 1.0, 0.0)
    extra = jnp.where(
        lane == o,
        nh,
        jnp.where(lane == o + 1, nm, jnp.where(lane == o + 2, nl, ones)),
    )
    return (xf * scale).astype(BF), extra.astype(BF)


def kernel(n, idx_ref, x_ref, v_ref, o_ref, xe, xl, ve, vl, oext, fext, vs,
           ring_send, ring_recv, sib_send, sib_recv):
    rows, width = x_ref.shape
    half = rows // 2
    chips = n // 2
    depth = chips // 2
    me = lax.axis_index("dp")
    chip, core = me // 2, me % 2

    z, y = chip // 2, chip % 2
    pos = (1 - y) * z + y * (chips - 1 - z)

    def device_at(q, c):
        q = lax.rem(q + 2 * chips, chips)
        second = q // depth
        qz = (1 - second) * q + second * (chips - 1 - q)
        return (qz * 2 + second) * 2 + c

    right, left = device_at(pos + 1, core), device_at(pos - 1, core)
    sibling = device_at(pos, 1 - core)

    barrier = pltpu.get_barrier_semaphore()
    for other in (right, left, sibling):
        pl.semaphore_signal(
            barrier, inc=1, device_id={"dp": other}, device_id_type=pl.DeviceIdType.MESH
        )

    def remote(src, dst, send, recv, to):
        return pltpu.make_async_remote_copy(
            src_ref=src, dst_ref=dst, send_sem=send, recv_sem=recv,
            device_id={"dp": to}, device_id_type=pl.DeviceIdType.MESH,
        )

    def slots(direction, distance):
        early = distance <= depth if direction == 0 else distance < depth
        return (xe, ve) if early else (xl, vl)

    def own_half(h):
        return (x_ref.at[pl.ds(h * half, half), :], v_ref.at[:, pl.ds(h * half, half)])

    pending = []

    def ring(direction, step):
        sign = 1 - 2 * direction
        blk = device_at(pos - sign * step, core)
        if step == 0:
            source = own_half(direction)
        else:
            bx, bv = slots(direction, step)
            source = (bx.at[blk], bv.at[blk])
        dx, dv = slots(direction, step + 1)
        to = right if direction == 0 else left
        out = []
        for k, (s, d) in enumerate(zip(source, (dx, dv))):
            c = remote(s, d.at[blk], ring_send.at[direction, step, k],
                       ring_recv.at[direction, step, k], to)
            c.start()
            out.append(c)
            pending.append(c)
        return out

    def pass_on(direction, step):
        sign = 1 - 2 * direction
        blk = device_at(pos - sign * step, core)
        if step == 0:
            source = own_half(direction)
            dx, dv = (xe, ve) if direction == 0 else (xl, vl)
        else:
            dx, dv = slots(direction, step)
            source = (dx.at[blk], dv.at[blk])
        out = []
        for k, (s, d) in enumerate(zip(source, (dx, dv))):
            c = remote(s, d.at[blk], sib_send.at[direction, step, k],
                       sib_recv.at[direction, step, k], sibling)
            c.start()
            out.append(c)
            pending.append(c)
        return out

    pl.semaphore_wait(barrier, 3)
    moving = [ring(0, 0), ring(1, 0)]
    from_sibling = [pass_on(0, 0), pass_on(1, 0)]

    def advance(step):
        for direction in range(2):
            for c in moving[direction]:
                c.wait_recv()
            if step < chips - 1:
                moving[direction] = ring(direction, step)
            from_sibling.append(pass_on(direction, step))

    def sibling_done():
        for copies in from_sibling:
            for c in copies:
                c.wait_recv()
        from_sibling.clear()

    chunk = 256

    def far(load):
        def step(c, carry):
            r = pl.ds(pl.multiple_of(c * chunk, chunk), chunk)
            a, b = extended(load(r), 1.0, False)
            fext[r, 0:width] = a
            fext[r, width:] = b
            return carry

        lax.fori_loop(0, half // chunk, step, 0)

    def product(first=0, last=rows // BLOCK_I):
        def istep(i, carry):
            ri = pl.ds(pl.multiple_of(i * BLOCK_I, BLOCK_I), BLOCK_I)
            s = lax.dot_general(
                fext[...], oext[ri, :], (((1,), (1,)), ((), ())), preferred_element_type=F32
            )
            k = jnp.exp(s).astype(BF)
            o_ref[:, ri] += jnp.dot(vs[...], k, preferred_element_type=F32)
            return carry

        lax.fori_loop(first, last, istep, 0)

    def tile(bx, bv, i):
        far(lambda r: bx[i, r, :])
        vs[...] = bv[i]
        product()

    def own_step(c, carry):
        r = pl.ds(pl.multiple_of(c * chunk, chunk), chunk)
        a, b = extended(x_ref[r, :], 2 * GAMMA, True)
        oext[r, 0:width] = a
        oext[r, width:] = b
        return carry

    lax.fori_loop(0, rows // chunk, own_step, 0)
    o_ref[...] = NOISE * v_ref[...].astype(F32)

    def own_tile(h):
        far(lambda r: x_ref[pl.ds(pl.multiple_of(r.start + h * half, chunk), chunk), :])
        vs[...] = v_ref[:, h * half:(h + 1) * half]
        product()

    own_tile(0)
    advance(1)
    own_tile(1)
    for step in range(2, depth + 1):
        advance(step)
    sibling_done()
    across = device_at(pos + depth, 1 - core)
    first, second = idx_ref[0], idx_ref[1]
    work = [
        lambda: tile(xe, ve, across),
        lambda: tile(xl, vl, across),
        lambda: tile(xe, ve, first),
        lambda: tile(xe, ve, second),
    ]
    for step in range(depth + 1, chips):
        if work:
            work.pop(0)()
        advance(step)
    for todo in work:
        todo()
    sibling_done()
    tile(xl, vl, first)
    tile(xl, vl, second)
    for c in pending:
        c.wait_send()


def on_device(n, points, probes, round_masks):
    rows, width = points.shape
    probe_count = probes.shape[0]
    me = lax.axis_index("dp")
    low = jnp.min(round_masks)
    mid = jnp.sum(round_masks) - low - jnp.max(round_masks)
    idx = jnp.bitwise_xor(me, jnp.stack([low, mid]))
    chips = n // 2
    vmem = pl.BlockSpec(memory_space=pltpu.VMEM)
    dots = 4 * rows * rows
    return pl.pallas_call(
        functools.partial(kernel, n),
        out_shape=jax.ShapeDtypeStruct((probe_count, rows), F32),
        in_specs=[pl.BlockSpec(memory_space=pltpu.SMEM), vmem, vmem],
        out_specs=vmem,
        scratch_shapes=[
            pltpu.VMEM((n, rows // 2, width), BF),
            pltpu.VMEM((n, rows // 2, width), BF),
            pltpu.VMEM((n, probe_count, rows // 2), BF),
            pltpu.VMEM((n, probe_count, rows // 2), BF),
            pltpu.VMEM((rows, width + 128), BF),
            pltpu.VMEM((rows // 2, width + 128), BF),
            pltpu.VMEM((probe_count, rows // 2), BF),
            pltpu.SemaphoreType.DMA((2, chips - 1, 2)),
            pltpu.SemaphoreType.DMA((2, chips - 1, 2)),
            pltpu.SemaphoreType.DMA((2, chips, 2)),
            pltpu.SemaphoreType.DMA((2, chips, 2)),
        ],
        compiler_params=pltpu.CompilerParams(
            collective_id=0, has_side_effects=True, vmem_limit_bytes=60 << 20
        ),
        cost_estimate=pl.CostEstimate(
            flops=2 * dots * (width + 16), bytes_accessed=2 * rows * width, transcendentals=dots
        ),
    )(idx, points, probes)


def solution(mesh):
    in_specs = (P(("groups", "dp"), None), P(None, ("groups", "dp")), P("groups"))
    out_specs = P(None, ("groups", "dp"))
    return jax.shard_map(
        functools.partial(on_device, mesh.shape["dp"]),
        mesh=mesh, in_specs=in_specs, out_specs=out_specs, check_vma=False,
    )
```

```python
import functools

import jax
import jax.numpy as jnp
from jax import lax
from jax.experimental import pallas as pl
from jax.experimental.pallas import tpu as pltpu
from jax.sharding import PartitionSpec as P

GAMMA = 2.0
NOISE = 0.25
F32, BF = jnp.float32, jnp.bfloat16
BLOCK_I = 1024
PIECES = 2


def extended(x, scale, own):
    xf = x.astype(F32)
    n = -GAMMA * jnp.sum(xf * xf, axis=1, keepdims=True)
    nh = n.astype(BF).astype(F32)
    rest = n - nh
    nm = rest.astype(BF).astype(F32)
    nl = rest - nm
    lane = lax.broadcasted_iota(jnp.int32, (x.shape[0], 128), 1)
    o = 0 if own else 3
    p = 3 - o
    ones = jnp.where((lane >= p) & (lane < p + 3), 1.0, 0.0)
    extra = jnp.where(
        lane == o,
        nh,
        jnp.where(lane == o + 1, nm, jnp.where(lane == o + 2, nl, ones)),
    )
    return (xf * scale).astype(BF), extra.astype(BF)


def kernel(n, idx_ref, x_ref, v_ref, o_ref, xe, xl, ve, vl, oext, fext, vs,
           ring_send, ring_recv, sib_send, sib_recv):
    rows, width = x_ref.shape
    half = rows // 2
    part = half // PIECES
    chips = n // 2
    depth = chips // 2
    me = lax.axis_index("dp")
    chip, core = me // 2, me % 2

    z, y = chip // 2, chip % 2
    pos = (1 - y) * z + y * (chips - 1 - z)

    def device_at(q, c):
        q = lax.rem(q + 2 * chips, chips)
        second = q // depth
        qz = (1 - second) * q + second * (chips - 1 - q)
        return (qz * 2 + second) * 2 + c

    right, left = device_at(pos + 1, core), device_at(pos - 1, core)
    sibling = device_at(pos, 1 - core)

    barrier = pltpu.get_barrier_semaphore()
    for other in (right, left, sibling):
        pl.semaphore_signal(
            barrier, inc=1, device_id={"dp": other}, device_id_type=pl.DeviceIdType.MESH
        )

    def remote(src, dst, send, recv, to):
        return pltpu.make_async_remote_copy(
            src_ref=src, dst_ref=dst, send_sem=send, recv_sem=recv,
            device_id={"dp": to}, device_id_type=pl.DeviceIdType.MESH,
        )

    def slots(direction, distance):
        early = distance <= depth if direction == 0 else distance < depth
        return (xe, ve) if early else (xl, vl)

    def piece(h, k):
        at = h * half + k * part
        return x_ref.at[pl.ds(at, part), :], v_ref.at[:, pl.ds(at, part)]

    def held(refs, blk, k):
        bx, bv = refs
        return bx.at[blk, pl.ds(k * part, part), :], bv.at[blk, :, pl.ds(k * part, part)]

    pending = []

    def send(source, target, sends, recvs, at, to):
        out = []
        for j, (s, d) in enumerate(zip(source, target)):
            c = remote(s, d, sends.at[at + (j,)], recvs.at[at + (j,)], to)
            c.start()
            out.append(c)
            pending.append(c)
        return out

    def block_back(direction, step):
        return device_at(pos - (1 - 2 * direction) * step, core)

    def ring(direction, step, k):
        blk = block_back(direction, step)
        source = piece(direction, k) if step == 0 else held(slots(direction, step), blk, k)
        target = held(slots(direction, step + 1), blk, k)
        return send(source, target, ring_send, ring_recv, (direction, step, k),
                    left if direction else right)

    def pass_on(direction, step, k):
        blk = block_back(direction, step)
        if step == 0:
            source, refs = piece(direction, k), (xl, vl) if direction else (xe, ve)
        else:
            refs = slots(direction, step)
            source = held(refs, blk, k)
        return send(source, held(refs, blk, k), sib_send, sib_recv, (direction, step, k), sibling)

    pl.semaphore_wait(barrier, 3)
    pieces = [(k, direction) for k in range(PIECES) for direction in range(2)]
    moving = {(k, direction): ring(direction, 0, k) for k, direction in pieces}
    from_sibling = [pass_on(direction, 0, k) for k, direction in pieces]

    def advance(step):
        for k, direction in pieces:
            for c in moving[k, direction]:
                c.wait_recv()
            if step < chips - 1:
                moving[k, direction] = ring(direction, step, k)
            from_sibling.append(pass_on(direction, step, k))

    def sibling_done():
        for copies in from_sibling:
            for c in copies:
                c.wait_recv()
        from_sibling.clear()

    chunk = 256

    def far(load):
        def step(c, carry):
            r = pl.ds(pl.multiple_of(c * chunk, chunk), chunk)
            a, b = extended(load(r), 1.0, False)
            fext[r, 0:width] = a
            fext[r, width:] = b
            return carry

        lax.fori_loop(0, half // chunk, step, 0)

    def product(first=0, last=rows // BLOCK_I):
        def istep(i, carry):
            ri = pl.ds(pl.multiple_of(i * BLOCK_I, BLOCK_I), BLOCK_I)
            s = lax.dot_general(
                fext[...], oext[ri, :], (((1,), (1,)), ((), ())), preferred_element_type=F32
            )
            k = jnp.exp(s).astype(BF)
            o_ref[:, ri] += jnp.dot(vs[...], k, preferred_element_type=F32)
            return carry

        lax.fori_loop(first, last, istep, 0)

    def tile(bx, bv, i):
        far(lambda r: bx[i, r, :])
        vs[...] = bv[i]
        product()

    def own_step(c, carry):
        r = pl.ds(pl.multiple_of(c * chunk, chunk), chunk)
        a, b = extended(x_ref[r, :], 2 * GAMMA, True)
        oext[r, 0:width] = a
        oext[r, width:] = b
        return carry

    lax.fori_loop(0, rows // chunk, own_step, 0)
    o_ref[...] = NOISE * v_ref[...].astype(F32)

    def own_tile(h):
        far(lambda r: x_ref[pl.ds(pl.multiple_of(r.start + h * half, chunk), chunk), :])
        vs[...] = v_ref[:, h * half:(h + 1) * half]
        product()

    own_tile(0)
    advance(1)
    own_tile(1)
    for step in range(2, depth + 1):
        advance(step)
    sibling_done()
    across = device_at(pos + depth, 1 - core)
    first, second = idx_ref[0], idx_ref[1]
    work = [
        lambda: tile(xe, ve, across),
        lambda: tile(xl, vl, across),
        lambda: tile(xe, ve, first),
        lambda: tile(xe, ve, second),
    ]
    for step in range(depth + 1, chips):
        if work:
            work.pop(0)()
        advance(step)
    for todo in work:
        todo()
    sibling_done()
    tile(xl, vl, first)
    tile(xl, vl, second)
    for c in pending:
        c.wait_send()


def on_device(n, points, probes, round_masks):
    rows, width = points.shape
    probe_count = probes.shape[0]
    me = lax.axis_index("dp")
    low = jnp.min(round_masks)
    mid = jnp.sum(round_masks) - low - jnp.max(round_masks)
    idx = jnp.bitwise_xor(me, jnp.stack([low, mid]))
    chips = n // 2
    vmem = pl.BlockSpec(memory_space=pltpu.VMEM)
    dots = 4 * rows * rows
    return pl.pallas_call(
        functools.partial(kernel, n),
        out_shape=jax.ShapeDtypeStruct((probe_count, rows), F32),
        in_specs=[pl.BlockSpec(memory_space=pltpu.SMEM), vmem, vmem],
        out_specs=vmem,
        scratch_shapes=[
            pltpu.VMEM((n, rows // 2, width), BF),
            pltpu.VMEM((n, rows // 2, width), BF),
            pltpu.VMEM((n, probe_count, rows // 2), BF),
            pltpu.VMEM((n, probe_count, rows // 2), BF),
            pltpu.VMEM((rows, width + 128), BF),
            pltpu.VMEM((rows // 2, width + 128), BF),
            pltpu.VMEM((probe_count, rows // 2), BF),
            pltpu.SemaphoreType.DMA((2, chips - 1, PIECES, 2)),
            pltpu.SemaphoreType.DMA((2, chips - 1, PIECES, 2)),
            pltpu.SemaphoreType.DMA((2, chips, PIECES, 2)),
            pltpu.SemaphoreType.DMA((2, chips, PIECES, 2)),
        ],
        compiler_params=pltpu.CompilerParams(
            collective_id=0, has_side_effects=True, vmem_limit_bytes=60 << 20
        ),
        cost_estimate=pl.CostEstimate(
            flops=2 * dots * (width + 16), bytes_accessed=2 * rows * width, transcendentals=dots
        ),
    )(idx, points, probes)


def solution(mesh):
    in_specs = (P(("groups", "dp"), None), P(None, ("groups", "dp")), P("groups"))
    out_specs = P(None, ("groups", "dp"))
    return jax.shard_map(
        functools.partial(on_device, mesh.shape["dp"]),
        mesh=mesh, in_specs=in_specs, out_specs=out_specs, check_vma=False,
    )
```
